512 devices in a mesh: row: 8 (over z_lo), inst: 16 (over y, z_hi, core), cell: 4 (over x).
Axes of the slice: x: 4, y: 4, z: 16 (z_hi: 2, z_lo: 8; z = z_hi * 8 + z_lo), core: 2. Of those that a mesh axis runs over, the one named last changes fastest.
Arguments:
- base_state: float32 [4, 64, 512, 512], P(None, 'inst', 'row', 'cell'), as said below
- segment_state: float32 [4, 64, 512, 512], P(None, 'inst', 'row', 'cell'), as said below
- spectral: float32 [8, 64, 64], P('row'), as said below
- donors: int32 [8, 2, 64, 2], P('row'), may hold values from 0 to 63, as said below
- donor_weight: float32 [8, 2, 64], P('row'), may hold values from 0 to 1
Outputs:
- new_state: float32 [4, 64, 512, 512], P(None, 'inst', 'row', 'cell')
- residual: float32 [4, 64, 512, 512], P(None, 'inst', 'row', 'cell')
The draws below stay inside these ranges and needn't reach their ends.
Inputs may be any that keep to these rules, and one draw needn't show every extreme that they name: Every cell and slot of base_state and segment_state holds a state (rho, rho u, rho v, E) with rho between 0.75 and 1.25 and pressure between 0.35 and 0.95. `segment_state`: as for base_state. spectral[s] is the frequency of blade row b(s) times the spectral time-derivative matrix over its first n(s) slots, zero in all other rows and columns; sections of one blade row have equal matrices. Side 0 refers to section s-1, side 1 to section s+1. Where that section belongs to another blade row and j < n(s), both donors are slots below that row's count; otherwise both donors equal j.
All inputs are finite; a program needn't handle non-finite values.
Results may differ from the reference program's by a relative error of at most 0.0003.
Values sent between devices are 32-bit elements; how exact they have to be, the bound alone decides.
No kernel may reach another device: no remote copies, remote signals or barrier semaphores. Data moves between devices by JAX's collectives and lax.ppermute only.
A program may use at most 64 MiB of HBM per device.

```python
import math
import jax
import jax.numpy as jnp
from jax import lax

NV = 4
NI = 64
AX_DEV = 64
SECTIONS = 8
AX = 512
PITCH = 512


def blade_of(index, sections):
    return (index >= sections // 4).astype(jnp.int32) + (index >= 3 * sections // 4).astype(jnp.int32)


def count_of(blade_row):
    return jnp.where(blade_row == 0, 45, jnp.where(blade_row == 1, 64, 55)).astype(jnp.int32)


def flow_state(key):
    shape = (NI, AX, PITCH)
    keys = jax.random.split(key, 4)
    density = 1.0 + 0.25 * jax.random.uniform(keys[0], shape, jnp.float32, -1.0, 1.0)
    axial_vel = 0.5 + 0.25 * jax.random.uniform(keys[1], shape, jnp.float32, -1.0, 1.0)
    cross_vel = 0.25 * jax.random.uniform(keys[2], shape, jnp.float32, -1.0, 1.0)
    pressure = (1.0 + 0.3 * jax.random.uniform(keys[3], shape, jnp.float32, -1.0, 1.0)) / 1.4
    energy = pressure / 0.4 + 0.5 * density * (axial_vel * axial_vel + cross_vel * cross_vel)
    return jnp.stack([density, density * axial_vel, density * cross_vel, energy]).astype(jnp.float32)


def draw_base_state(key, part):
    return flow_state(jax.random.fold_in(key, 11))


def draw_segment_state(key, part):
    return flow_state(jax.random.fold_in(key, 23))


def draw_spectral(key, part):
    keys = jax.random.split(jax.random.fold_in(key, 37), 2)
    rates = jnp.exp(jax.random.uniform(keys[1], (3,), jnp.float32, math.log(0.05), math.log(0.2)))
    section = jnp.arange(SECTIONS, dtype=jnp.int32)
    blade_row = blade_of(section, SECTIONS)
    active = count_of(blade_row)[:, None, None]
    rate = rates[blade_row][:, None, None]
    target = jnp.arange(NI, dtype=jnp.int32)[None, :, None]
    source = jnp.arange(NI, dtype=jnp.int32)[None, None, :]
    offset = target - source
    inside = (target < active) & (source < active) & (offset != 0)
    parity = 1.0 - 2.0 * (jnp.abs(offset) % 2).astype(jnp.float32)
    angle = jnp.where(inside, math.pi * offset.astype(jnp.float32) / active.astype(jnp.float32), 0.5 * math.pi)
    factor = jnp.where(active % 2 == 0, jnp.cos(angle) / jnp.sin(angle), 1.0 / jnp.sin(angle))
    return jnp.where(inside, 0.5 * rate * parity * factor, 0.0).astype(jnp.float32)


def draw_donors(key, part):
    section = jnp.arange(SECTIONS, dtype=jnp.int32)[:, None]
    side = jnp.arange(2, dtype=jnp.int32)[None, :]
    neighbour = section - 1 + 2 * side
    inside = (neighbour >= 0) & (neighbour < SECTIONS)
    own_blade = blade_of(section, SECTIONS)
    other_blade = blade_of(jnp.clip(neighbour, 0, SECTIONS - 1), SECTIONS)
    interface = inside & (own_blade != other_blade)
    own_count = count_of(own_blade)[:, :, None] + jnp.zeros((1, 2, 1), jnp.int32)
    source_count = count_of(other_blade)[:, :, None]
    target = jnp.arange(NI, dtype=jnp.int32)[None, None, :]
    picks = jax.random.randint(jax.random.fold_in(key, 53), (SECTIONS, 2, NI), 0, source_count)
    picks = jnp.where(target == own_count - 1, source_count - 1, picks)
    used = interface[:, :, None] & (target < own_count)
    donor_low = jnp.where(used, picks, target)
    donor_high = jnp.where(used, (picks + 1) % source_count, target)
    return jnp.stack([donor_low, donor_high], axis=-1).astype(jnp.int32)


def block_levels(stream_key, shape, shards, low, high):
    gain = 1.0
    for position, blocks in shards:
        heights = jax.random.uniform(jax.random.fold_in(jax.random.fold_in(stream_key, 6), position), (blocks,), jnp.float32, low / len(shards), high / len(shards))
        gain = gain * jnp.repeat(jnp.exp(heights), shape[position] // blocks).reshape((-1,) + (1,) * (len(shape) - 1 - position))
    return gain


def setup_inputs(seed: int = 0) -> dict:
    key_list = jax.random.split(jax.random.key(seed), 6)
    base_state = draw_base_state(jax.random.fold_in(key_list[5], 71), 0)
    segment_state = draw_segment_state(jax.random.fold_in(key_list[5], 71), 0)
    spectral = draw_spectral(jax.random.fold_in(key_list[5], 71), 0)
    donors = draw_donors(jax.random.fold_in(key_list[5], 71), 0)
    donor_weight = jnp.clip(1.0 * jax.random.uniform(key_list[4], (SECTIONS, 2, NI), jnp.float32) ** block_levels(key_list[4], (SECTIONS, 2, NI), ((0, 8),), -0.2, 0.2), 0.0, 1.0)
    return dict(base_state=base_state, segment_state=segment_state, spectral=spectral, donors=donors, donor_weight=donor_weight)


heat_ratio = 1.4
courant = 0.8
segment_coeff = 0.5

def primitives(conserved):
    density = conserved[0]
    axial_vel = conserved[1] / density
    cross_vel = conserved[2] / density
    pressure = (heat_ratio - 1.0) * (conserved[3] - 0.5 * density * (axial_vel * axial_vel + cross_vel * cross_vel))
    return (density, axial_vel, cross_vel, pressure)

def roe_flux(left_state, right_state):
    dens_left, norm_left, tang_left, pres_left = primitives(left_state)
    dens_right, norm_right, tang_right, pres_right = primitives(right_state)
    enth_left = (left_state[3] + pres_left) / dens_left
    enth_right = (right_state[3] + pres_right) / dens_right
    root_left = jnp.sqrt(dens_left)
    root_right = jnp.sqrt(dens_right)
    weight = 1.0 / (root_left + root_right)
    norm_avg = (root_left * norm_left + root_right * norm_right) * weight
    tang_avg = (root_left * tang_left + root_right * tang_right) * weight
    enth_avg = (root_left * enth_left + root_right * enth_right) * weight
    dens_avg = root_left * root_right
    kinetic = 0.5 * (norm_avg * norm_avg + tang_avg * tang_avg)
    celerity_sq = (heat_ratio - 1.0) * (enth_avg - kinetic)
    celerity = jnp.sqrt(celerity_sq)
    jump_dens = dens_right - dens_left
    jump_norm = norm_right - norm_left
    jump_tang = tang_right - tang_left
    jump_pres = pres_right - pres_left
    wave_one = (jump_pres - dens_avg * celerity * jump_norm) / (2.0 * celerity_sq)
    wave_four = (jump_pres + dens_avg * celerity * jump_norm) / (2.0 * celerity_sq)
    wave_two = jump_dens - jump_pres / celerity_sq
    wave_three = dens_avg * jump_tang
    speed_one = jnp.abs(norm_avg - celerity) * wave_one
    speed_two = jnp.abs(norm_avg) * wave_two
    speed_three = jnp.abs(norm_avg) * wave_three
    speed_four = jnp.abs(norm_avg + celerity) * wave_four
    mass_left = dens_left * norm_left
    mass_right = dens_right * norm_right
    acoustic = speed_one + speed_two + speed_four
    flux_mass = 0.5 * (mass_left + mass_right) - 0.5 * acoustic
    flux_norm = 0.5 * (mass_left * norm_left + pres_left + mass_right * norm_right + pres_right) - 0.5 * (speed_one * (norm_avg - celerity) + speed_two * norm_avg + speed_four * (norm_avg + celerity))
    flux_tang = 0.5 * (mass_left * tang_left + mass_right * tang_right) - 0.5 * (acoustic * tang_avg + speed_three)
    flux_energy = 0.5 * (mass_left * enth_left + mass_right * enth_right) - 0.5 * (speed_one * (enth_avg - norm_avg * celerity) + speed_two * kinetic + speed_three * tang_avg + speed_four * (enth_avg + norm_avg * celerity))
    return jnp.stack([flux_mass, flux_norm, flux_tang, flux_energy])

def reorder(conserved):
    return jnp.stack([conserved[0], conserved[2], conserved[1], conserved[3]])

def blade_counts(sections):
    section = jnp.arange(sections, dtype=jnp.int32)
    blade_row = (section >= sections // 4).astype(jnp.int32) + (section >= 3 * sections // 4).astype(jnp.int32)
    return jnp.where(blade_row == 0, 45, jnp.where(blade_row == 1, 64, 55)).astype(jnp.int32)

def reference(base_state, segment_state, spectral, donors, donor_weight):
    highest = lax.Precision.HIGHEST
    columns = jnp.arange(NI, dtype=jnp.int32)
    donor_low = donors[..., 0]
    donor_high = donors[..., 1]
    resample = (1.0 - donor_weight)[..., None] * (columns == donor_low[..., None]).astype(jnp.float32) + donor_weight[..., None] * (columns == donor_high[..., None]).astype(jnp.float32)
    blocks = segment_state.reshape(NV, NI, SECTIONS, AX_DEV, PITCH)
    first_rows = blocks[:, :, :, 0]
    last_rows = blocks[:, :, :, -1]
    zero_edge = jnp.zeros_like(first_rows[:, :, :1])
    from_up = jnp.concatenate([zero_edge, last_rows[:, :, :-1]], axis=2)
    from_down = jnp.concatenate([first_rows[:, :, 1:], zero_edge], axis=2)
    ghost_up = jnp.einsum('sjl,vlsp->vjsp', resample[:, 0], from_up, precision=highest)
    ghost_down = jnp.einsum('sjl,vlsp->vjsp', resample[:, 1], from_down, precision=highest)
    edge_index = jnp.arange(SECTIONS, dtype=jnp.int32)[None, None, :, None]
    ghost_up = jnp.where(edge_index == 0, first_rows, ghost_up)
    ghost_down = jnp.where(edge_index == SECTIONS - 1, last_rows, ghost_down)

    def spatial_one(inputs):
        field, upper_edge, lower_edge = inputs
        extended = jnp.concatenate([upper_edge[:, :, None], field, lower_edge[:, :, None]], axis=2)
        axial_flux = roe_flux(extended[:, :, :-1], extended[:, :, 1:])
        axial_net = axial_flux[:, :, 1:] - axial_flux[:, :, :-1]
        ahead = jnp.roll(field, -1, axis=-1)
        face_flux = reorder(roe_flux(reorder(field), reorder(ahead)))
        pitch_net = face_flux - jnp.roll(face_flux, 1, axis=-1)
        return axial_net + pitch_net
    spatial = lax.map(spatial_one, (jnp.moveaxis(blocks, 1, 0), jnp.moveaxis(ghost_up, 1, 0), jnp.moveaxis(ghost_down, 1, 0)))
    spatial = jnp.moveaxis(spatial, 0, 1)
    temporal = jnp.einsum('sjl,vlsap->vjsap', spectral, blocks, precision=highest)
    live_mask = (columns[:, None] < blade_counts(SECTIONS)[None, :])[None, :, :, None, None]
    residual = jnp.where(live_mask, temporal + spatial, 0.0)
    density, axial_vel, cross_vel, pressure = primitives(blocks)
    celerity = jnp.sqrt(heat_ratio * pressure / density)
    time_step = courant / (jnp.abs(axial_vel) + jnp.abs(cross_vel) + 2.0 * celerity)
    updated = base_state.reshape(NV, NI, SECTIONS, AX_DEV, PITCH) - segment_coeff * time_step * residual
    return (updated.reshape(NV, NI, AX, PITCH), residual.reshape(NV, NI, AX, PITCH))
```

```python
import jax
import jax.numpy as jnp
from jax import lax
from jax.experimental import pallas as pl
from jax.experimental.pallas import tpu as pltpu
from jax.sharding import PartitionSpec as P

heat_ratio = 1.4
courant = 0.8
segment_coeff = 0.5

GROUPS = [[y * 4 + half * 2 + c for y in range(4) for c in range(2)] for half in range(2)]
PARTNER = [(i, i ^ 2) for i in range(16)]
INTERFACE = (1, 2, 5, 6)
VMEM = pl.BlockSpec(memory_space=pltpu.VMEM)
SMEM = pl.BlockSpec(memory_space=pltpu.SMEM)


def swap_members(value):
    return lax.all_to_all(value, "inst", 0, 0, tiled=True, axis_index_groups=GROUPS)


def primitives(dens, mom_norm, mom_tang, energy):
    inverse = 1.0 / dens
    norm = mom_norm * inverse
    tang = mom_tang * inverse
    pres = (heat_ratio - 1.0) * (energy - 0.5 * (mom_norm * norm + mom_tang * tang))
    enth = (energy + pres) * inverse
    return (dens, norm, tang, pres, enth, jnp.sqrt(dens), mom_norm)


def roe(left, right):
    dens_l, norm_l, tang_l, pres_l, enth_l, root_l, mass_l = left
    dens_r, norm_r, tang_r, pres_r, enth_r, root_r, mass_r = right
    weight = 1.0 / (root_l + root_r)
    share_l = root_l * weight
    share_r = root_r * weight
    norm = share_l * norm_l + share_r * norm_r
    tang = share_l * tang_l + share_r * tang_r
    enth = share_l * enth_l + share_r * enth_r
    dens = root_l * root_r
    kinetic = 0.5 * (norm * norm + tang * tang)
    cel_sq = (heat_ratio - 1.0) * (enth - kinetic)
    cel = jnp.sqrt(cel_sq)
    inverse = 1.0 / cel_sq
    jump_pres = pres_r - pres_l
    push = dens * cel * (norm_r - norm_l)
    half_inverse = 0.5 * inverse
    one = jnp.abs(norm - cel) * ((jump_pres - push) * half_inverse)
    four = jnp.abs(norm + cel) * ((jump_pres + push) * half_inverse)
    speed = jnp.abs(norm)
    two = speed * ((dens_r - dens_l) - jump_pres * inverse)
    three = speed * (dens * (tang_r - tang_l))
    outer = one + four
    acoustic = outer + two
    spread = cel * (four - one)
    flux_mass = 0.5 * (mass_l + mass_r - acoustic)
    flux_norm = 0.5 * (mass_l * norm_l + pres_l + mass_r * norm_r + pres_r - (acoustic * norm + spread))
    flux_tang = 0.5 * (mass_l * tang_l + mass_r * tang_r - (acoustic * tang + three))
    flux_energy = 0.5 * (
        mass_l * enth_l + mass_r * enth_r - (outer * enth + norm * spread + two * kinetic + three * tang)
    )
    return flux_mass, flux_norm, flux_tang, flux_energy


def operator_rows(matrix, source, first_row, variables, begin, store):
    for pair in range(4):
        targets = [(member, i) for member in (2 * pair, 2 * pair + 1) for i in range(4)]

        def body(member, sums):
            sums = list(sums)
            for i in range(4):
                tiles = [source[member, pl.ds(first_row + (v * 4 + i) * 8, 8), :] for v in range(variables)]
                for k, (tm, ti) in enumerate(targets):
                    factor = matrix[tm * 4 + ti, member * 4 + i]
                    for v in range(variables):
                        sums[k * variables + v] = sums[k * variables + v] + factor * tiles[v]
            return tuple(sums)

        start = tuple(begin(tm, v, ti) for tm, ti in targets for v in range(variables))
        sums = lax.fori_loop(0, 8, body, start)
        for k, (tm, ti) in enumerate(targets):
            for v in range(variables):
                store(tm, v, ti, sums[k * variables + v])


def outgoing_kernel(matrix, source, out):
    def store(member, v, i, tile):
        out[member, pl.ds((v * 4 + i) * 8, 8), :] = tile

    operator_rows(matrix, source, 64, 2, lambda *_: jnp.zeros((8, 128), jnp.float32), store)


def own_kernel(matrix, source, out):
    for first in (0, 64):

        def store(member, v, i, tile, first=first):
            out[member, pl.ds(first + (v * 4 + i) * 8, 8), :] = tile

        operator_rows(matrix, source, first, 2, lambda *_: jnp.zeros((8, 128), jnp.float32), store)


def arrived_kernel(matrix, resample, own, source, out):
    def begin(member, v, i):
        return own[member, pl.ds((v * 4 + i) * 8, 8), :]

    def store(member, v, i, tile):
        out[member, pl.ds((v * 4 + i) * 8, 8), :] = tile

    operator_rows(matrix, source, 0, 2, begin, store)
    for member in range(8):
        out[member, 64:128, :] = own[member, 64:128, :]
    edges = source[:, 64:72, :].reshape(64, 128)
    ghost = jnp.dot(resample[...], edges, precision=lax.Precision.HIGHEST, preferred_element_type=jnp.float32)
    out[:, 128:136, :] = ghost.reshape(8, 8, 128)


def spatial_kernel(state, sides, out, step, prims):
    lane = lax.broadcasted_iota(jnp.int32, (8, 128), 1)
    row = lax.broadcasted_iota(jnp.int32, (8, 128), 0)
    columns = sides[0].T
    for o in range(8):
        at = slice(8 * o, 8 * o + 8)
        cells = [state[v, 0, at, :] for v in range(4)]
        dens, norm, tang, pres, enth, root, _ = primitives(*cells)
        cel = jnp.sqrt(heat_ratio * pres / dens)
        step[0, at, :] = (segment_coeff * courant) / (jnp.abs(norm) + jnp.abs(tang) + 2.0 * cel)
        for k, value in enumerate((dens, norm, tang, pres, enth, root, cells[1], cells[2])):
            prims[k, at, :] = value
    previous = None
    for o in range(8):
        at = slice(8 * o, 8 * o + 8)
        here = [prims[k, at, :] for k in range(8)]
        if o < 7:
            below = [prims[k, 8 * o + 1 : 8 * o + 9, :] for k in range(8)]
        else:
            below = [pltpu.roll(x, 7, 0) for x in here]
        axial = roe([here[k] for k in (0, 1, 2, 3, 4, 5, 6)], [below[k] for k in (0, 1, 2, 3, 4, 5, 6)])
        if o == 7:
            axial = [jnp.where(row == 7, 0.0, x) for x in axial]
        ahead = [pltpu.roll(x, 127, 1) for x in here]
        mass, tang, norm, energy = roe(
            [here[k] for k in (0, 2, 1, 3, 4, 5, 7)], [ahead[k] for k in (0, 2, 1, 3, 4, 5, 7)]
        )
        pitch = (mass, norm, tang, energy)
        shifted = [pltpu.roll(x, 1, 0) for x in axial]
        for v in range(4):
            above = 0.0 if previous is None else jnp.broadcast_to(previous[v][0:1, :], (8, 128))
            net = axial[v] - jnp.where(row == 0, above, shifted[v])
            first = jnp.broadcast_to(columns[at, 2 * v : 2 * v + 1], (8, 128))
            last = jnp.broadcast_to(columns[at, 2 * v + 1 : 2 * v + 2], (8, 128))
            after = jnp.where(lane == 127, last, pitch[v])
            before = jnp.where(lane == 0, first, pltpu.roll(pitch[v], 1, 1))
            out[v, 0, at, :] = net + (after - before)
        previous = shifted


def final_kernel(facts, base, state, spatial, step, local, crossed, new_state, residual):
    row = lax.broadcasted_iota(jnp.int32, (8, 128), 0)
    first_rows = [state[v, :, 0, :] for v in range(4)]
    last_rows = [state[v, :, 63, :] for v in range(4)]
    up = [jnp.where(facts[1] == 1, first_rows[v], local[2 * v, 128:132, :]) for v in range(4)]
    down = [jnp.where(facts[2] == 1, last_rows[v], local[2 * v + 1, 128:132, :]) for v in range(4)]
    flux_up = roe(primitives(*up), primitives(*first_rows))
    flux_down = roe(primitives(*last_rows), primitives(*down))
    for i in range(4):
        live = facts[0] > i
        for o in range(8):
            at = slice(8 * o, 8 * o + 8)
            factor = step[i, at, :]
            for v in range(4):
                rows = slice((v * 4 + i) * 8, (v * 4 + i) * 8 + 8)
                total = spatial[v, i, at, :] + local[o, rows, :]
                if v >= 2:
                    total = total + crossed[o, slice(rows.start - 64, rows.stop - 64), :]
                if o == 0:
                    edge = jnp.broadcast_to(flux_up[v][i : i + 1, :], (8, 128))
                    total = total - jnp.where(row == 0, edge, 0.0)
                if o == 7:
                    edge = jnp.broadcast_to(flux_down[v][i : i + 1, :], (8, 128))
                    total = total + jnp.where(row == 7, edge, 0.0)
                total = jnp.where(live, total, 0.0)
                residual[v, i, at, :] = total
                new_state[v, i, at, :] = base[v, i, at, :] - factor * total


def shape(*dims):
    return jax.ShapeDtypeStruct(dims, jnp.float32)


def cost(flops, moved):
    return pl.CostEstimate(flops=flops, bytes_accessed=moved, transcendentals=0)


def per_device(base_state, segment_state, spectral, donors, donor_weight):
    section = lax.axis_index("row")
    inst = lax.axis_index("inst")
    half = (inst // 2) % 2
    member = (inst // 4) * 2 + inst % 2
    blade_row = (section >= 2).astype(jnp.int32) + (section >= 6).astype(jnp.int32)
    active = jnp.where(blade_row == 0, 45, jnp.where(blade_row == 1, 64, 55))
    facts = jnp.stack([active - 4 * inst, (section == 0).astype(jnp.int32), (section == 7).astype(jnp.int32)])

    blocks = spectral[0].reshape(4, 2, 8, 4, 2, 8)
    low_low, low_high, high_low, high_high = [
        blocks[:, a, :, :, b, :].reshape(32, 32) for a in range(2) for b in range(2)
    ]
    own_own = jnp.where(half == 0, low_low, high_high)
    own_partner = jnp.where(half == 0, low_high, high_low)
    partner_own = jnp.where(half == 0, high_low, low_high)

    side = member % 2
    pairs = jnp.where(side == 0, donors[0, 0], donors[0, 1]).reshape(4, 2, 2, 4, 2)
    pairs = jnp.where(half == 0, pairs[:, 0], pairs[:, 1]).reshape(8, 4, 2)
    part = jnp.where(side == 0, donor_weight[0, 0], donor_weight[0, 1]).reshape(4, 2, 2, 4)
    part = jnp.where(half == 0, part[:, 0], part[:, 1]).reshape(8, 4)
    k = jnp.arange(64, dtype=jnp.int32)
    source_member, relative, source_i = k // 8, (k // 4) % 2, k % 4
    slots = (source_member // 2) * 16 + (half ^ relative) * 8 + (source_member % 2) * 4 + source_i
    resample = (1.0 - part)[..., None] * (slots == pairs[..., 0, None]).astype(jnp.float32) + part[..., None] * (
        slots == pairs[..., 1, None]
    ).astype(jnp.float32)
    resample = jnp.pad(resample, ((0, 0), (0, 4), (0, 0))).reshape(64, 64)

    octets = segment_state.reshape(4, 4, 8, 8, 128).transpose(2, 0, 1, 3, 4).reshape(8, 128, 128)
    mixed = swap_members(octets)
    raw_half = octets[:, :64]
    arrived_half = lax.ppermute(raw_half, "inst", PARTNER)

    first_row = segment_state[:, :, 0, :]
    last_row = segment_state[:, :, 63, :]
    upward = [(i, i + 1) for i in range(7)]
    downward = [(i + 1, i) for i in range(7)]
    from_up = lax.ppermute(last_row, "row", upward)
    from_down = lax.ppermute(first_row, "row", downward)
    edges = jnp.stack([from_up, from_down], axis=1).reshape(8, 4, 128)
    partner_edges = lax.ppermute(
        edges, ("row", "inst"), [(r * 16 + a, r * 16 + b) for r in INTERFACE for a, b in PARTNER]
    )

    outgoing = pl.pallas_call(
        outgoing_kernel, out_shape=shape(8, 64, 128), in_specs=[SMEM, VMEM], out_specs=VMEM,
        cost_estimate=cost(4 << 20, 1 << 20), name="outgoing",
    )(partner_own, mixed)
    crossed = lax.ppermute(swap_members(outgoing), "inst", PARTNER)
    own = pl.pallas_call(
        own_kernel, out_shape=shape(8, 128, 128), in_specs=[SMEM, VMEM], out_specs=VMEM,
        cost_estimate=cost(8 << 20, 1 << 20), name="own",
    )(own_own, mixed)

    first_column = segment_state[..., 0]
    last_column = segment_state[..., 127]
    around = [(i, (i + 1) % 4) for i in range(4)]
    from_left = lax.ppermute(last_column, "cell", around)
    from_right = lax.ppermute(first_column, "cell", [(b, a) for a, b in around])

    def swapped(x):
        return primitives(x[0], x[2], x[1], x[3])

    faces = []
    for left, right in ((from_left, first_column), (last_column, from_right)):
        mass, tang, norm, energy = roe(swapped(left), swapped(right))
        faces.append(jnp.stack([mass, norm, tang, energy]))
    sides = jnp.stack(faces, axis=1).transpose(2, 0, 1, 3).reshape(4, 8, 64)
    sides = jnp.pad(sides, ((0, 0), (0, 0), (0, 64)))
    spatial, step = pl.pallas_call(
        spatial_kernel,
        grid=(4,),
        out_shape=(shape(4, 4, 64, 128), shape(4, 64, 128)),
        in_specs=[
            pl.BlockSpec((4, 1, 64, 128), lambda i: (0, i, 0, 0)),
            pl.BlockSpec((1, 8, 128), lambda i: (i, 0, 0)),
        ],
        out_specs=(
            pl.BlockSpec((4, 1, 64, 128), lambda i: (0, i, 0, 0)),
            pl.BlockSpec((1, 64, 128), lambda i: (i, 0, 0)),
        ),
        scratch_shapes=[pltpu.VMEM((8, 64, 128), jnp.float32)],
        cost_estimate=cost(16 << 20, 2 << 20), name="spatial",
    )(segment_state, sides)

    second = swap_members(jnp.concatenate([arrived_half, edges, partner_edges], axis=1))
    totals = pl.pallas_call(
        arrived_kernel, out_shape=shape(8, 136, 128), in_specs=[SMEM, VMEM, VMEM, VMEM], out_specs=VMEM,
        cost_estimate=cost(4 << 20, 1 << 20), name="arrived",
    )(own_partner, resample, own, second)
    local = swap_members(totals)
    return pl.pallas_call(
        final_kernel,
        out_shape=(shape(4, 4, 64, 128), shape(4, 4, 64, 128)),
        in_specs=[SMEM] + [VMEM] * 6,
        out_specs=(VMEM, VMEM),
        cost_estimate=cost(1 << 20, 4 << 20), name="final",
    )(facts, base_state, segment_state, spatial, step, local, crossed)


def solution(mesh):
    placed = (
        P(None, "inst", "row", "cell"),
        P(None, "inst", "row", "cell"),
        P("row", None, None),
        P("row", None, None, None),
        P("row", None, None),
    )
    return jax.shard_map(
        per_device,
        mesh=mesh,
        in_specs=placed,
        out_specs=(P(None, "inst", "row", "cell"), P(None, "inst", "row", "cell")),
        check_vma=False,
    )
```

```python
import jax
import jax.numpy as jnp
from jax import lax
from jax.experimental import pallas as pl
from jax.experimental.pallas import tpu as pltpu
from jax.sharding import PartitionSpec as P

heat_ratio = 1.4
courant = 0.8
segment_coeff = 0.5

GROUPS = [[y * 4 + half * 2 + c for y in range(4) for c in range(2)] for half in range(2)]
PARTNER = [(i, i ^ 2) for i in range(16)]
VMEM = pl.BlockSpec(memory_space=pltpu.VMEM)
SMEM = pl.BlockSpec(memory_space=pltpu.SMEM)


def swap_members(value):
    return lax.all_to_all(value, "inst", 0, 0, tiled=True, axis_index_groups=GROUPS)


def primitives(dens, mom_norm, mom_tang, energy):
    inverse = 1.0 / dens
    norm = mom_norm * inverse
    tang = mom_tang * inverse
    pres = (heat_ratio - 1.0) * (energy - 0.5 * (mom_norm * norm + mom_tang * tang))
    enth = (energy + pres) * inverse
    return (dens, norm, tang, pres, enth, jnp.sqrt(dens), mom_norm)


def roe(left, right):
    dens_l, norm_l, tang_l, pres_l, enth_l, root_l, mass_l = left
    dens_r, norm_r, tang_r, pres_r, enth_r, root_r, mass_r = right
    weight = 1.0 / (root_l + root_r)
    share_l = root_l * weight
    share_r = root_r * weight
    norm = share_l * norm_l + share_r * norm_r
    tang = share_l * tang_l + share_r * tang_r
    enth = share_l * enth_l + share_r * enth_r
    dens = root_l * root_r
    kinetic = 0.5 * (norm * norm + tang * tang)
    cel_sq = (heat_ratio - 1.0) * (enth - kinetic)
    cel = jnp.sqrt(cel_sq)
    inverse = 1.0 / cel_sq
    jump_pres = pres_r - pres_l
    push = dens * cel * (norm_r - norm_l)
    half_inverse = 0.5 * inverse
    one = jnp.abs(norm - cel) * ((jump_pres - push) * half_inverse)
    four = jnp.abs(norm + cel) * ((jump_pres + push) * half_inverse)
    speed = jnp.abs(norm)
    two = speed * ((dens_r - dens_l) - jump_pres * inverse)
    three = speed * (dens * (tang_r - tang_l))
    outer = one + four
    acoustic = outer + two
    spread = cel * (four - one)
    flux_mass = 0.5 * (mass_l + mass_r - acoustic)
    flux_norm = 0.5 * (mass_l * norm_l + pres_l + mass_r * norm_r + pres_r - (acoustic * norm + spread))
    flux_tang = 0.5 * (mass_l * tang_l + mass_r * tang_r - (acoustic * tang + three))
    flux_energy = 0.5 * (
        mass_l * enth_l + mass_r * enth_r - (outer * enth + norm * spread + two * kinetic + three * tang)
    )
    return flux_mass, flux_norm, flux_tang, flux_energy


def place():
    inst = lax.axis_index("inst")
    return lax.axis_index("row"), inst, lax.rem(inst // 2, 2), (inst // 4) * 2 + lax.rem(inst, 2)


def place():
    inst = lax.axis_index("inst")
    return lax.axis_index("row"), inst, lax.rem(inst // 2, 2), (inst // 4) * 2 + lax.rem(inst, 2)


def wide_rows(ref, offset, stride, count=32):
    return jnp.concatenate([ref[pl.ds(offset + r, count, stride=stride), :] for r in range(8)], axis=1)


def parts(value):
    high = value.astype(jnp.bfloat16)
    return high, (value - high.astype(jnp.float32)).astype(jnp.bfloat16)


def half_rows(matrix, half):
    return jnp.concatenate(
        [matrix[pl.ds(pl.multiple_of(y * 16 + half * 8, 8), 8), :] for y in range(4)], axis=0
    )


def left_factor(rows, source_half):
    slot = lax.broadcasted_iota(jnp.int32, (64, 96), 0)
    column = lax.broadcasted_iota(jnp.int32, (64, 96), 1)
    place_in = lax.rem(column, 32)
    picked = slot == (place_in // 8) * 16 + source_half * 8 + lax.rem(place_in, 8)
    middle = (column >= 32) & (column < 64)
    zero, one = jnp.zeros((64, 96), jnp.float32), jnp.ones((64, 96), jnp.float32)
    pick_high = jnp.where(picked, jnp.where(middle, zero, one), zero).astype(jnp.bfloat16)
    pick_low = jnp.where(picked, jnp.where(middle, one, zero), zero).astype(jnp.bfloat16)
    high, low = parts(rows)
    both = jnp.dot(high, pick_high, preferred_element_type=jnp.float32) + jnp.dot(
        low, pick_low, preferred_element_type=jnp.float32
    )
    return both.astype(jnp.bfloat16)


def right_factor(value):
    high, low = parts(value)
    return jnp.concatenate([high, high, low], axis=0)


def split_kernel(state, octets, edges):
    for o in range(8):
        for i in range(4):
            for v in range(4):
                row = o * 128 + i * 32 + v * 8
                octets[row : row + 8, :] = state[v, i, 8 * o : 8 * o + 8, :]
    for v in range(4):
        edges[0, v] = state[v, :, 0, :]
        edges[1, v] = state[v, :, 63, :]


def outgoing_kernel(matrix, source, out):
    _, _, half, _ = place()
    lefts = [left_factor(half_rows(matrix, target_half), half) for target_half in (half, 1 - half)]
    for v in range(2):
        right = right_factor(wide_rows(source, (2 + v) * 8, 32))
        for k in range(2):
            total = jnp.dot(lefts[k], right, preferred_element_type=jnp.float32)
            for r in range(8):
                out[pl.ds(k * 16 + v * 8 + r, 32, stride=32), :] = total[:, r * 128 : r * 128 + 128]


def second_kernel(raw, up, down, partner, out):
    section, _, _, _ = place()
    from_above = (section == 2) | (section == 6)
    for o in range(8):
        v, own = o // 2, (up if o % 2 == 0 else down)
        mine = own[v]
        other = jnp.where(from_above if o % 2 == 0 else jnp.logical_not(from_above), partner[v], 0.0)
        for i in range(4):
            row = o * 72 + i * 18
            for p in range(2):
                out[row + p * 8 : row + p * 8 + 8, :] = raw[p, i, 8 * o : 8 * o + 8, :]
            out[row + 16 : row + 18, :] = jnp.concatenate([mine[i : i + 1], other[i : i + 1]], axis=0)


def arrived_kernel(matrix, resample, mixed, source, out):
    _, _, half, _ = place()
    rows = half_rows(matrix, half)
    own_left = left_factor(rows, half)
    other_left = left_factor(rows, 1 - half)
    for v in range(2):
        total = jnp.dot(own_left, right_factor(wide_rows(mixed, v * 8, 32)), preferred_element_type=jnp.float32)
        total = total + jnp.dot(
            other_left, right_factor(wide_rows(source, v * 8, 18)), preferred_element_type=jnp.float32
        )
        for r in range(8):
            out[pl.ds(v * 8 + r, 32, stride=18), :] = total[:, r * 128 : r * 128 + 128]
    weights = half_rows(resample, half)
    ghost = jnp.zeros((32, 128), jnp.float32)
    for k, source_half in enumerate((half, 1 - half)):
        edge = source[pl.ds(16 + k, 32, stride=18), :]
        ghost = ghost + jnp.dot(
            left_factor(weights, source_half), right_factor(edge), preferred_element_type=jnp.float32
        )
    for k in range(2):
        out[pl.ds(16 + k, 32, stride=18), :] = ghost


def spatial_kernel(state, first_column, last_column, from_left, from_right, out, step, prims, columns):
    lane = lax.broadcasted_iota(jnp.int32, (8, 128), 1)
    row = lax.broadcasted_iota(jnp.int32, (8, 128), 0)
    slot = pl.program_id(0)

    @pl.when(slot == 0)
    def _():
        faces = []
        for left, right in ((from_left, first_column), (last_column, from_right)):
            mass, tang, norm, energy = roe(
                primitives(*[left[v] for v in (0, 2, 1, 3)]), primitives(*[right[v] for v in (0, 2, 1, 3)])
            )
            faces.append((mass, norm, tang, energy))
        for i in range(4):
            rows = [faces[side][v][i : i + 1, :] for v in range(4) for side in range(2)]
            block = jnp.concatenate(rows, axis=0)
            columns[i] = jnp.concatenate([block, jnp.zeros((8, 64), jnp.float32)], axis=1).T

    for o in range(8):
        at = slice(8 * o, 8 * o + 8)
        cells = [state[v, 0, at, :] for v in range(4)]
        dens, norm, tang, pres, enth, root, _ = primitives(*cells)
        cel = jnp.sqrt(heat_ratio * pres / dens)
        step[0, at, :] = (segment_coeff * courant) / (jnp.abs(norm) + jnp.abs(tang) + 2.0 * cel)
        for k, value in enumerate((dens, norm, tang, pres, enth, root, cells[1], cells[2])):
            prims[k, at, :] = value
    previous = None
    for o in range(8):
        at = slice(8 * o, 8 * o + 8)
        here = [prims[k, at, :] for k in range(8)]
        if o < 7:
            below = [prims[k, 8 * o + 1 : 8 * o + 9, :] for k in range(8)]
        else:
            below = [pltpu.roll(x, 7, 0) for x in here]
        axial = roe(here[:7], below[:7])
        if o == 7:
            axial = [jnp.where(row == 7, 0.0, x) for x in axial]
        ahead = [pltpu.roll(x, 127, 1) for x in here]
        mass, tang, norm, energy = roe(
            [here[k] for k in (0, 2, 1, 3, 4, 5, 7)], [ahead[k] for k in (0, 2, 1, 3, 4, 5, 7)]
        )
        pitch = (mass, norm, tang, energy)
        shifted = [pltpu.roll(x, 1, 0) for x in axial]
        sides = columns[slot, at, :]
        for v in range(4):
            above = 0.0 if previous is None else jnp.broadcast_to(previous[v][0:1, :], (8, 128))
            net = axial[v] - jnp.where(row == 0, above, shifted[v])
            first = jnp.broadcast_to(sides[:, 2 * v : 2 * v + 1], (8, 128))
            last = jnp.broadcast_to(sides[:, 2 * v + 1 : 2 * v + 2], (8, 128))
            after = jnp.where(lane == 127, last, pitch[v])
            before = jnp.where(lane == 0, first, pltpu.roll(pitch[v], 1, 1))
            out[v, 0, at, :] = net + (after - before)
        previous = shifted


def final_kernel(base, edges, spatial, step, local, own, crossed, new_state, residual):
    section, inst, _, _ = place()
    active = jnp.where(section < 2, 45, jnp.where(section < 6, 64, 55))
    row = lax.broadcasted_iota(jnp.int32, (8, 128), 0)
    first_rows = [edges[0, v] for v in range(4)]
    last_rows = [edges[1, v] for v in range(4)]
    ghosts = [local[pl.ds(k * 72 + 16, 4, stride=18), :] for k in range(8)]
    up = [jnp.where(section == 0, first_rows[v], ghosts[2 * v]) for v in range(4)]
    down = [jnp.where(section == 7, last_rows[v], ghosts[2 * v + 1]) for v in range(4)]
    flux_up = roe(primitives(*up), primitives(*first_rows))
    flux_down = roe(primitives(*last_rows), primitives(*down))
    for i in range(4):
        live = inst * 4 + i < active
        for o in range(8):
            at = slice(8 * o, 8 * o + 8)
            factor = step[i, at, :]
            for v in range(4):
                total = spatial[v, i, at, :]
                if v < 2:
                    row_at = o * 72 + i * 18 + v * 8
                    total = total + local[row_at : row_at + 8, :]
                else:
                    rows = slice(v * 8 - 16, v * 8 - 8)
                    total = total + (own[o * 4 + i, rows, :] + crossed[o * 4 + i, rows, :])
                if o == 0:
                    edge = jnp.broadcast_to(flux_up[v][i : i + 1, :], (8, 128))
                    total = total - jnp.where(row == 0, edge, 0.0)
                if o == 7:
                    edge = jnp.broadcast_to(flux_down[v][i : i + 1, :], (8, 128))
                    total = total + jnp.where(row == 7, edge, 0.0)
                total = jnp.where(live, total, 0.0)
                residual[v, i, at, :] = total
                new_state[v, i, at, :] = base[v, i, at, :] - factor * total


def shape(*dims):
    return jax.ShapeDtypeStruct(dims, jnp.float32)


SMALL = pl.CostEstimate(flops=1000, bytes_accessed=1000, transcendentals=0)


def call(kernel, name, estimate, *operands, **options):
    return pl.pallas_call(kernel, name=name, cost_estimate=estimate, **options)(*operands)


def staged(needed, stage, *operands):
    given = jax.eval_shape(stage, *operands)
    return lax.cond(needed, stage, lambda *_: jax.tree.map(lambda x: jnp.zeros(x.shape, x.dtype), given), *operands)


def per_device(base_state, segment_state, spectral, donors, donor_weight):
    section, inst, _, member = place()
    matrix = spectral[0]
    needed = inst < 16

    def leave(state, matrix):
        arrived_half = lax.ppermute(state[:2], "inst", PARTNER)
        octets, edge_rows = call(
            split_kernel, "split", SMALL, state,
            out_shape=(shape(1024, 128), shape(2, 4, 4, 128)), in_specs=[VMEM], out_specs=(VMEM, VMEM),
        )
        mixed = swap_members(octets)
        from_up = lax.ppermute(edge_rows[1], "row", [(i, i + 1) for i in range(7)])
        from_down = lax.ppermute(edge_rows[0], "row", [(i + 1, i) for i in range(7)])
        meeting = [(1, 2), (2, 1), (5, 6), (6, 5)]
        partner_edges = lax.ppermute(
            jnp.where((section == 1) | (section == 5), edge_rows[1], edge_rows[0]),
            ("row", "inst"),
            [(r * 16 + a, s * 16 + b) for r, s in meeting for a, b in PARTNER],
        )
        outgoing = call(
            outgoing_kernel, "outgoing", SMALL, matrix, mixed,
            out_shape=shape(1024, 128), in_specs=[VMEM] * 2, out_specs=VMEM,
        )
        first_column = state[..., 0]
        last_column = state[..., 127]
        around = [(i, (i + 1) % 4) for i in range(4)]
        from_left = lax.ppermute(last_column, "cell", around)
        from_right = lax.ppermute(first_column, "cell", [(b, a) for a, b in around])
        returned = swap_members(outgoing).reshape(32, 32, 128)
        columns = (first_column, last_column, from_left, from_right)
        return arrived_half, mixed, returned, returned[:, 16:], edge_rows, from_up, from_down, partner_edges, columns

    arrived_half, mixed, returned, crossing, edge_rows, from_up, from_down, partner_edges, columns = staged(
        needed, leave, segment_state, matrix
    )
    crossed = lax.ppermute(crossing, "inst", PARTNER)

    side = lax.rem(member, 2)
    slots = jnp.arange(64, dtype=jnp.int32)
    donor = jnp.where(side == 0, donors[0, 0], donors[0, 1])
    weight = jnp.where(side == 0, donor_weight[0, 0], donor_weight[0, 1])[:, None]
    resample = (1.0 - weight) * (slots == donor[:, :1]).astype(jnp.float32) + weight * (
        slots == donor[:, 1:]
    ).astype(jnp.float32)

    def arrive(state, matrix, resample, mixed, raw, up, down, partner, columns):
        second = call(
            second_kernel, "second", SMALL, raw, up, down, partner,
            out_shape=shape(576, 128), in_specs=[VMEM] * 4, out_specs=VMEM,
        )
        totals = call(
            arrived_kernel, "arrived", SMALL, matrix, resample, mixed, swap_members(second),
            out_shape=shape(576, 128), in_specs=[VMEM] * 4, out_specs=VMEM,
        )
        slot_block = pl.BlockSpec((4, 1, 64, 128), lambda i: (0, i, 0, 0))
        spatial, step = call(
            spatial_kernel, "spatial", SMALL, state, *columns,
            grid=(4,),
            out_shape=(shape(4, 4, 64, 128), shape(4, 64, 128)),
            in_specs=[slot_block] + [pl.BlockSpec((4, 4, 64), lambda i: (0, 0, 0))] * 4,
            out_specs=(slot_block, pl.BlockSpec((1, 64, 128), lambda i: (i, 0, 0))),
            scratch_shapes=[pltpu.VMEM((8, 64, 128), jnp.float32), pltpu.VMEM((4, 128, 8), jnp.float32)],
        )
        return swap_members(totals), spatial, step

    local, spatial, step = staged(
        needed, arrive,
        segment_state, matrix, resample, mixed, arrived_half, from_up, from_down, partner_edges, columns,
    )
    whole = pl.BlockSpec((4, 4, 64, 128), lambda _: (0, 0, 0, 0))
    sums = pl.BlockSpec((32, 16, 128), lambda _: (0, 0, 0))
    return call(
        final_kernel, "final", SMALL, base_state, edge_rows, spatial, step, local, returned, crossed,
        grid=(1,),
        out_shape=(shape(4, 4, 64, 128), shape(4, 4, 64, 128)),
        in_specs=[
            whole, pl.BlockSpec((2, 4, 4, 128), lambda _: (0, 0, 0, 0)), whole,
            pl.BlockSpec((4, 64, 128), lambda _: (0, 0, 0)), pl.BlockSpec((576, 128), lambda _: (0, 0)), sums, sums,
        ],
        out_specs=(whole, whole),
    )


def solution(mesh):
    placed = (
        P(None, "inst", "row", "cell"),
        P(None, "inst", "row", "cell"),
        P("row", None, None),
        P("row", None, None, None),
        P("row", None, None),
    )
    return jax.shard_map(
        per_device,
        mesh=mesh,
        in_specs=placed,
        out_specs=(P(None, "inst", "row", "cell"), P(None, "inst", "row", "cell")),
        check_vma=False,
    )
```

```python
import jax
import jax.numpy as jnp
from jax import lax
from jax.experimental import pallas as pl
from jax.experimental.pallas import tpu as pltpu
from jax.sharding import PartitionSpec as P

heat_ratio = 1.4
courant = 0.8
segment_coeff = 0.5

GROUPS = [[y * 4 + half * 2 + c for y in range(4) for c in range(2)] for half in range(2)]
PARTNER = [(i, i ^ 2) for i in range(16)]
VMEM = pl.BlockSpec(memory_space=pltpu.VMEM)
SMEM = pl.BlockSpec(memory_space=pltpu.SMEM)


def swap_members(value):
    return lax.all_to_all(value, "inst", 0, 0, tiled=True, axis_index_groups=GROUPS)


def primitives(dens, mom_norm, mom_tang, energy):
    inverse = 1.0 / dens
    norm = mom_norm * inverse
    tang = mom_tang * inverse
    pres = (heat_ratio - 1.0) * (energy - 0.5 * (mom_norm * norm + mom_tang * tang))
    enth = (energy + pres) * inverse
    return (dens, norm, tang, pres, enth, jnp.sqrt(dens), mom_norm)


def roe(left, right):
    dens_l, norm_l, tang_l, pres_l, enth_l, root_l, mass_l = left
    dens_r, norm_r, tang_r, pres_r, enth_r, root_r, mass_r = right
    weight = 1.0 / (root_l + root_r)
    share_l = root_l * weight
    share_r = root_r * weight
    norm = share_l * norm_l + share_r * norm_r
    tang = share_l * tang_l + share_r * tang_r
    enth = share_l * enth_l + share_r * enth_r
    dens = root_l * root_r
    kinetic = 0.5 * (norm * norm + tang * tang)
    cel_sq = (heat_ratio - 1.0) * (enth - kinetic)
    cel = jnp.sqrt(cel_sq)
    inverse = 1.0 / cel_sq
    jump_pres = pres_r - pres_l
    push = dens * cel * (norm_r - norm_l)
    half_inverse = 0.5 * inverse
    one = jnp.abs(norm - cel) * ((jump_pres - push) * half_inverse)
    four = jnp.abs(norm + cel) * ((jump_pres + push) * half_inverse)
    speed = jnp.abs(norm)
    two = speed * ((dens_r - dens_l) - jump_pres * inverse)
    three = speed * (dens * (tang_r - tang_l))
    outer = one + four
    acoustic = outer + two
    spread = cel * (four - one)
    flux_mass = 0.5 * (mass_l + mass_r - acoustic)
    flux_norm = 0.5 * (mass_l * norm_l + pres_l + mass_r * norm_r + pres_r - (acoustic * norm + spread))
    flux_tang = 0.5 * (mass_l * tang_l + mass_r * tang_r - (acoustic * tang + three))
    flux_energy = 0.5 * (
        mass_l * enth_l + mass_r * enth_r - (outer * enth + norm * spread + two * kinetic + three * tang)
    )
    return flux_mass, flux_norm, flux_tang, flux_energy


def place():
    inst = lax.axis_index("inst")
    return lax.axis_index("row"), inst, lax.rem(inst // 2, 2), (inst // 4) * 2 + lax.rem(inst, 2)


def place():
    inst = lax.axis_index("inst")
    return lax.axis_index("row"), inst, lax.rem(inst // 2, 2), (inst // 4) * 2 + lax.rem(inst, 2)


def wide_rows(ref, offset, stride, count=32):
    return jnp.concatenate([ref[pl.ds(offset + r, count, stride=stride), :] for r in range(8)], axis=1)


def parts(value):
    high = value.astype(jnp.bfloat16)
    return high, (value - high.astype(jnp.float32)).astype(jnp.bfloat16)


def half_rows(matrix, half):
    return jnp.concatenate(
        [matrix[pl.ds(pl.multiple_of(y * 16 + half * 8, 8), 8), :] for y in range(4)], axis=0
    )


def left_factor(rows, source_half):
    slot = lax.broadcasted_iota(jnp.int32, (64, 96), 0)
    column = lax.broadcasted_iota(jnp.int32, (64, 96), 1)
    place_in = lax.rem(column, 32)
    picked = slot == (place_in // 8) * 16 + source_half * 8 + lax.rem(place_in, 8)
    middle = (column >= 32) & (column < 64)
    zero, one = jnp.zeros((64, 96), jnp.float32), jnp.ones((64, 96), jnp.float32)
    pick_high = jnp.where(picked, jnp.where(middle, zero, one), zero).astype(jnp.bfloat16)
    pick_low = jnp.where(picked, jnp.where(middle, one, zero), zero).astype(jnp.bfloat16)
    high, low = parts(rows)
    both = jnp.dot(high, pick_high, preferred_element_type=jnp.float32) + jnp.dot(
        low, pick_low, preferred_element_type=jnp.float32
    )
    return both.astype(jnp.bfloat16)


def right_factor(value):
    high, low = parts(value)
    return jnp.concatenate([high, high, low], axis=0)


def split_kernel(state, octets, edges):
    for o in range(8):
        for i in range(4):
            for v in range(4):
                row = o * 128 + i * 32 + v * 8
                octets[row : row + 8, :] = state[v, i, 8 * o : 8 * o + 8, :]
    for v in range(4):
        edges[0, v] = state[v, :, 0, :]
        edges[1, v] = state[v, :, 63, :]


def pack_half_kernel(mixed, *rest):
    out = rest[-1]
    for k in range(32):
        out[k * 16 : k * 16 + 16, :] = mixed[k * 32 : k * 32 + 16, :]


def outgoing_kernel(matrix, source, up, down, partner, out):
    section, _, half, _ = place()
    from_above = (section == 2) | (section == 6)
    left = left_factor(half_rows(matrix, 1 - half), half)
    for v in range(2):
        total = jnp.dot(left, right_factor(wide_rows(source, (2 + v) * 8, 32)), preferred_element_type=jnp.float32)
        for r in range(8):
            out[pl.ds(v * 8 + r, 32, stride=18), :] = total[:, r * 128 : r * 128 + 128]
    for m in range(8):
        mine = (up if m % 2 == 0 else down)[m // 2]
        other = jnp.where(from_above if m % 2 == 0 else jnp.logical_not(from_above), partner[m // 2], 0.0)
        for i in range(4):
            row = (m * 4 + i) * 18 + 16
            out[row : row + 2, :] = jnp.concatenate([mine[i : i + 1], other[i : i + 1]], axis=0)


def pack_kernel(returned, *rest):
    out = rest[-1]
    for k in range(32):
        out[k * 16 : k * 16 + 16, :] = returned[k * 18 : k * 18 + 16, :]


def arrived_kernel(matrix, resample, mixed, returned, source, out):
    _, _, half, _ = place()
    rows = half_rows(matrix, half)
    own_left = left_factor(rows, half)
    other_left = left_factor(rows, 1 - half)
    for v in range(4):
        total = jnp.dot(own_left, right_factor(wide_rows(mixed, v * 8, 32)), preferred_element_type=jnp.float32)
        if v < 2:
            total = total + jnp.dot(
                other_left, right_factor(wide_rows(source, v * 8, 16)), preferred_element_type=jnp.float32
            )
        for r in range(8):
            out[pl.ds(v * 8 + r, 32, stride=34), :] = total[:, r * 128 : r * 128 + 128]
    weights = half_rows(resample, half)
    ghost = jnp.zeros((32, 128), jnp.float32)
    for k, source_half in enumerate((half, 1 - half)):
        edge = right_factor(returned[pl.ds(16 + k, 32, stride=18), :])
        ghost = ghost + jnp.dot(left_factor(weights, source_half), edge, preferred_element_type=jnp.float32)
    for k in range(2):
        out[pl.ds(32 + k, 32, stride=34), :] = ghost


def spatial_kernel(state, first_column, last_column, from_left, from_right, out, step, prims, columns):
    lane = lax.broadcasted_iota(jnp.int32, (8, 128), 1)
    row = lax.broadcasted_iota(jnp.int32, (8, 128), 0)
    slot = pl.program_id(0)

    @pl.when(slot == 0)
    def _():
        faces = []
        for left, right in ((from_left, first_column), (last_column, from_right)):
            mass, tang, norm, energy = roe(
                primitives(*[left[v] for v in (0, 2, 1, 3)]), primitives(*[right[v] for v in (0, 2, 1, 3)])
            )
            faces.append((mass, norm, tang, energy))
        for i in range(4):
            rows = [faces[side][v][i : i + 1, :] for v in range(4) for side in range(2)]
            block = jnp.concatenate(rows, axis=0)
            columns[i] = jnp.concatenate([block, jnp.zeros((8, 64), jnp.float32)], axis=1).T

    for o in range(8):
        at = slice(8 * o, 8 * o + 8)
        cells = [state[v, 0, at, :] for v in range(4)]
        dens, norm, tang, pres, enth, root, _ = primitives(*cells)
        cel = jnp.sqrt(heat_ratio * pres / dens)
        step[0, at, :] = (segment_coeff * courant) / (jnp.abs(norm) + jnp.abs(tang) + 2.0 * cel)
        for k, value in enumerate((dens, norm, tang, pres, enth, root, cells[1], cells[2])):
            prims[k, at, :] = value
    previous = None
    for o in range(8):
        at = slice(8 * o, 8 * o + 8)
        here = [prims[k, at, :] for k in range(8)]
        if o < 7:
            below = [prims[k, 8 * o + 1 : 8 * o + 9, :] for k in range(8)]
        else:
            below = [pltpu.roll(x, 7, 0) for x in here]
        axial = roe(here[:7], below[:7])
        if o == 7:
            axial = [jnp.where(row == 7, 0.0, x) for x in axial]
        ahead = [pltpu.roll(x, 127, 1) for x in here]
        mass, tang, norm, energy = roe(
            [here[k] for k in (0, 2, 1, 3, 4, 5, 7)], [ahead[k] for k in (0, 2, 1, 3, 4, 5, 7)]
        )
        pitch = (mass, norm, tang, energy)
        shifted = [pltpu.roll(x, 1, 0) for x in axial]
        sides = columns[slot, at, :]
        for v in range(4):
            above = 0.0 if previous is None else jnp.broadcast_to(previous[v][0:1, :], (8, 128))
            net = axial[v] - jnp.where(row == 0, above, shifted[v])
            first = jnp.broadcast_to(sides[:, 2 * v : 2 * v + 1], (8, 128))
            last = jnp.broadcast_to(sides[:, 2 * v + 1 : 2 * v + 2], (8, 128))
            after = jnp.where(lane == 127, last, pitch[v])
            before = jnp.where(lane == 0, first, pltpu.roll(pitch[v], 1, 1))
            out[v, 0, at, :] = net + (after - before)
        previous = shifted


def final_kernel(base, edges, spatial, step, local, crossed, new_state, residual):
    section, inst, _, _ = place()
    active = jnp.where(section < 2, 45, jnp.where(section < 6, 64, 55))
    row = lax.broadcasted_iota(jnp.int32, (8, 128), 0)
    first_rows = [edges[0, v] for v in range(4)]
    last_rows = [edges[1, v] for v in range(4)]
    ghosts = [local[pl.ds(k * 136 + 32, 4, stride=34), :] for k in range(8)]
    up = [jnp.where(section == 0, first_rows[v], ghosts[2 * v]) for v in range(4)]
    down = [jnp.where(section == 7, last_rows[v], ghosts[2 * v + 1]) for v in range(4)]
    flux_up = roe(primitives(*up), primitives(*first_rows))
    flux_down = roe(primitives(*last_rows), primitives(*down))
    for i in range(4):
        live = inst * 4 + i < active
        for o in range(8):
            at = slice(8 * o, 8 * o + 8)
            factor = step[i, at, :]
            for v in range(4):
                local_at, crossed_at = (o * 4 + i) * 34 + v * 8, (o * 4 + i) * 16 + v * 8 - 16
                total = spatial[v, i, at, :] + local[local_at : local_at + 8, :]
                if v >= 2:
                    total = total + crossed[crossed_at : crossed_at + 8, :]
                if o == 0:
                    edge = jnp.broadcast_to(flux_up[v][i : i + 1, :], (8, 128))
                    total = total - jnp.where(row == 0, edge, 0.0)
                if o == 7:
                    edge = jnp.broadcast_to(flux_down[v][i : i + 1, :], (8, 128))
                    total = total + jnp.where(row == 7, edge, 0.0)
                total = jnp.where(live, total, 0.0)
                residual[v, i, at, :] = total
                new_state[v, i, at, :] = base[v, i, at, :] - factor * total


def shape(*dims):
    return jax.ShapeDtypeStruct(dims, jnp.float32)


SMALL = pl.CostEstimate(flops=1000, bytes_accessed=1000, transcendentals=0)


def call(kernel, name, estimate, *operands, **options):
    return pl.pallas_call(kernel, name=name, cost_estimate=estimate, **options)(*operands)


def staged(needed, stage, *operands):
    given = jax.eval_shape(stage, *operands)
    return lax.cond(needed, stage, lambda *_: jax.tree.map(lambda x: jnp.zeros(x.shape, x.dtype), given), *operands)


def per_device(base_state, segment_state, spectral, donors, donor_weight):
    section, inst, _, member = place()
    matrix = spectral[0]
    needed = inst < 16
    anywhere = pl.BlockSpec(memory_space=pl.ANY)

    octets, edge_rows = call(
        split_kernel, "split", SMALL, segment_state,
        out_shape=(shape(1024, 128), shape(2, 4, 4, 128)), in_specs=[VMEM], out_specs=(VMEM, VMEM),
    )
    mixed = swap_members(octets)
    from_up = lax.ppermute(edge_rows[1], "row", [(i, i + 1) for i in range(7)])
    from_down = lax.ppermute(edge_rows[0], "row", [(i + 1, i) for i in range(7)])
    meeting = [(1, 2), (2, 1), (5, 6), (6, 5)]
    partner_edges = lax.ppermute(
        jnp.where((section == 1) | (section == 5), edge_rows[1], edge_rows[0]),
        ("row", "inst"),
        [(r * 16 + a, s * 16 + b) for r, s in meeting for a, b in PARTNER],
    )
    half = call(
        pack_half_kernel, "half", SMALL, mixed,
        out_shape=shape(512, 128), in_specs=[VMEM], out_specs=VMEM,
    )
    arrived_half = lax.ppermute(half, "inst", PARTNER)

    def leave(matrix, mixed, up, down, partner):
        outgoing = call(
            outgoing_kernel, "outgoing", SMALL, matrix, mixed, up, down, partner,
            out_shape=shape(576, 128), in_specs=[VMEM] * 5, out_specs=VMEM,
        )
        returned = swap_members(outgoing)
        crossing = call(
            pack_kernel, "pack", SMALL, returned, out_shape=shape(512, 128), in_specs=[VMEM], out_specs=VMEM,
        )
        return returned, crossing

    returned, crossing = staged(
        needed, leave, matrix, mixed, from_up, from_down, partner_edges
    )
    crossed = lax.ppermute(crossing, "inst", PARTNER)

    side = lax.rem(member, 2)
    slots = jnp.arange(64, dtype=jnp.int32)
    donor = jnp.where(side == 0, donors[0, 0], donors[0, 1])
    weight = jnp.where(side == 0, donor_weight[0, 0], donor_weight[0, 1])[:, None]
    resample = (1.0 - weight) * (slots == donor[:, :1]).astype(jnp.float32) + weight * (
        slots == donor[:, 1:]
    ).astype(jnp.float32)

    def arrive(state, matrix, resample, mixed, returned, arrived_half):
        first_column = state[..., 0]
        last_column = state[..., 127]
        around = [(i, (i + 1) % 4) for i in range(4)]
        from_left = lax.ppermute(last_column, "cell", around)
        from_right = lax.ppermute(first_column, "cell", [(b, a) for a, b in around])
        totals = call(
            arrived_kernel, "arrived", SMALL, matrix, resample, mixed, returned, arrived_half,
            out_shape=shape(1088, 128), in_specs=[VMEM] * 5, out_specs=VMEM,
        )
        slot_block = pl.BlockSpec((4, 1, 64, 128), lambda i: (0, i, 0, 0))
        spatial, step = call(
            spatial_kernel, "spatial", SMALL, state, first_column, last_column, from_left, from_right,
            grid=(4,),
            out_shape=(shape(4, 4, 64, 128), shape(4, 64, 128)),
            in_specs=[slot_block] + [pl.BlockSpec((4, 4, 64), lambda i: (0, 0, 0))] * 4,
            out_specs=(slot_block, pl.BlockSpec((1, 64, 128), lambda i: (i, 0, 0))),
            scratch_shapes=[pltpu.VMEM((8, 64, 128), jnp.float32), pltpu.VMEM((4, 128, 8), jnp.float32)],
        )
        return swap_members(totals), spatial, step

    local, spatial, step = staged(
        needed, arrive, segment_state, matrix, resample, mixed, returned, arrived_half
    )
    return call(
        final_kernel, "final", SMALL, base_state, edge_rows, spatial, step, local, crossed,
        out_shape=(shape(4, 4, 64, 128), shape(4, 4, 64, 128)),
        in_specs=[VMEM] * 6,
        out_specs=(VMEM, VMEM),
    )


def solution(mesh):
    placed = (
        P(None, "inst", "row", "cell"),
        P(None, "inst", "row", "cell"),
        P("row", None, None),
        P("row", None, None, None),
        P("row", None, None),
    )
    return jax.shard_map(
        per_device,
        mesh=mesh,
        in_specs=placed,
        out_specs=(P(None, "inst", "row", "cell"), P(None, "inst", "row", "cell")),
        check_vma=False,
    )
```
